512 devices in a mesh: partner: 32 (over y, x, core), block: 16 (over z).
Axes of the slice: x: 4, y: 4, z: 16, core: 2. Of those that a mesh axis runs over, the one named last changes fastest.
Arguments:
- points: bfloat16 [32, 524288], P(None, ('partner', 'block')), may hold values from -6 to 6
- tree_order: int32 [524288], P(('partner', 'block')), may hold values from 0 to 524287, as said below
- nearby_dense_blocks: bfloat16 [4096, 3, 128, 128], P(('partner', 'block')), may hold values from -0.3125 to 0.3125
- neighbours: int32 [4096, 3], P(('partner', 'block')), may hold values from 0 to 4095, as said below
- compress: bfloat16 [4096, 128, 128], P(('partner', 'block')), may hold values from -0.5 to 0.5
- expand: bfloat16 [4096, 128, 128], P(('partner', 'block')), may hold values from -0.5 to 0.5
- top_factor: bfloat16 [4096, 128, 128], P(('partner', 'block')), may hold values from -0.5 to 0.5
- butterfly_mixers: bfloat16 [4, 4096, 2, 128, 128], P(None, ('partner', 'block')), may hold values from -0.375 to 0.375
- block_map: int32 [5, 8], replicated, may hold values from 0 to 7, as said below
Outputs:
- applied: bfloat16 [32, 524288], P(None, ('partner', 'block'))
The draws below stay inside these ranges and needn't reach their ends.
Inputs may be any that keep to these rules, and one draw needn't show every extreme that they name: tree_order[r] lies among the 1024 points of the aligned group of 1024 rows that holds r, and names every point once. neighbours[l, 0] is l; every other entry lies within 2 leaves of l and in the same aligned group of 128 leaves as l. `block_map`: each row names exactly 4 different slots, each of them twice.
All inputs are finite; a program needn't handle non-finite values.
Results may differ from the reference program's by a relative error of at most 0.001.
Values may be sent and summed in bfloat16 or wider, within the bound.
A program may use at most 64 MiB of HBM per device.

```python
import jax
import jax.numpy as jnp
from jax import lax

NV = 32
LEAF = 128
KB = 128
NB = 3
REACH = 2
PTS_DEV = 1024
LEAVES_DEV = 8
LEVELS = 5
MIXS = 4
POINTS = 524288
LEAVES = 4096
N_PARTNER = 32
N_BLOCK = 16


def draw_tree_order(key, part):
    key = jax.random.fold_in(key, 11)
    devices = N_PARTNER * N_BLOCK
    keys = jax.random.split(key, devices)
    rows = jax.vmap(lambda single: jax.random.permutation(single, PTS_DEV))(keys)
    offsets = (jnp.arange(devices, dtype=jnp.int32) * PTS_DEV)[:, None]
    return (rows.astype(jnp.int32) + offsets).reshape(-1).astype(jnp.int32)


def draw_neighbours(key, part):
    key = jax.random.fold_in(key, 23)
    leaf_numbers = jnp.arange(LEAVES, dtype=jnp.int32)[:, None]
    span = LEAVES_DEV * N_BLOCK
    lowest = leaf_numbers // span * span
    offsets = jax.random.randint(key, (LEAVES, NB - 1), -REACH, REACH + 1, dtype=jnp.int32)
    others = jnp.clip(leaf_numbers + offsets, lowest, lowest + span - 1)
    return jnp.concatenate([leaf_numbers, others], axis=1).astype(jnp.int32)


def draw_block_map(key, part):
    key = jax.random.fold_in(key, 37)

    def one_row(single):
        first, second = jax.random.split(single)
        middle = 1 + jax.random.permutation(first, LEAVES_DEV - 2)[:LEAVES_DEV // 2 - 2]
        ends = jnp.array([0, LEAVES_DEV - 1], dtype=jnp.int32)
        chosen = jnp.concatenate([ends, middle.astype(jnp.int32)])
        doubled = jnp.concatenate([chosen, chosen])
        return jnp.take(doubled, jax.random.permutation(second, LEAVES_DEV))
    return jax.vmap(one_row)(jax.random.split(key, LEVELS)).astype(jnp.int32)


def shard_levels(rng, extent, shards, least, top_value):
    def one(dim, parts):
        heights = jax.random.uniform(jax.random.fold_in(jax.random.fold_in(rng, 6), dim), (parts,), jnp.float32, least / len(shards), top_value / len(shards))
        return jnp.repeat(jnp.exp(heights), extent[dim] // parts).reshape((-1,) + (1,) * (len(extent) - dim - 1))

    factor_of = one(*shards[0])
    for cut in shards[1:]:
        factor_of = factor_of * one(*cut)
    return factor_of


def normal_values(own_key, shape, spread, reach, cuts=(), kind=jnp.bfloat16):
    values = spread * jax.random.normal(own_key, shape, jnp.float32)
    if cuts:
        values = values * shard_levels(own_key, shape, cuts, -0.22, 0.18)
    return jnp.clip(values, -reach, reach).astype(kind)


def setup_inputs(seed: int = 0) -> dict:
    key_list = jax.random.split(jax.random.key(seed), 10)
    points = normal_values(key_list[0], (NV, POINTS), 1.0, 6.0, ((1, 512),))
    tree_order = draw_tree_order(jax.random.fold_in(key_list[9], 71), 0)
    nearby_dense_blocks = normal_values(key_list[2], (LEAVES, NB, LEAF, LEAF), (NB * LEAF) ** -0.5, 0.3125, ((0, 512),))
    neighbours = draw_neighbours(jax.random.fold_in(key_list[9], 71), 0)
    compress = normal_values(key_list[4], (LEAVES, LEAF, KB), LEAF ** -0.5, 0.5, ((0, 512),))
    expand = normal_values(key_list[5], (LEAVES, KB, LEAF), KB ** -0.5, 0.5, ((0, 512),))
    top_factor = normal_values(key_list[6], (LEAVES, KB, KB), KB ** -0.5, 0.5, ((0, 512),))
    butterfly_mixers = normal_values(key_list[7], (MIXS, LEAVES, 2, KB, KB), (2 * KB) ** -0.5, 0.375, ((1, 512),))
    block_map = draw_block_map(jax.random.fold_in(key_list[9], 71), 0)
    return dict(points=points, tree_order=tree_order, nearby_dense_blocks=nearby_dense_blocks, neighbours=neighbours, compress=compress, expand=expand, top_factor=top_factor, butterfly_mixers=butterfly_mixers, block_map=block_map)


HI = lax.Precision.HIGHEST


def swap_partner(state, bit):
    count = state.shape[0]
    grouped = state.reshape((count >> (bit + 1), 2, 1 << bit) + state.shape[1:])
    return jnp.flip(grouped, axis=1).reshape(state.shape)


def per_partner(func, *arrays):
    return lax.map(lambda pieces: func(*pieces), arrays)


def reference(points, tree_order, nearby_dense_blocks, neighbours, compress, expand, top_factor, butterfly_mixers, block_map):
    n_part = N_PARTNER
    n_blk = N_BLOCK
    ordered = jnp.take(points, tree_order, axis=0 + 1)
    leaf_rows = ordered.reshape(NV, LEAVES, LEAF).transpose(1, 0, 2)
    gathered = jnp.take(leaf_rows, neighbours.reshape(-1), axis=0).reshape(n_part, n_blk * LEAVES_DEV, NB, NV, LEAF)
    near_view = nearby_dense_blocks.reshape(n_part, n_blk * LEAVES_DEV, NB, LEAF, LEAF)

    def nearby_single_block(source, blocks):
        return jnp.einsum("lnvs,lnst->lvt", source.astype(jnp.float32), blocks.astype(jnp.float32))

    nearby_field_sum = per_partner(nearby_single_block, gathered, near_view).reshape(n_part, n_blk, LEAVES_DEV, NV, LEAF)

    own_rows = leaf_rows.reshape(n_part, n_blk, LEAVES_DEV, NV, LEAF)
    comp_view = compress.reshape(n_part, n_blk, LEAVES_DEV, LEAF, KB)

    def compress_one(rows, factor):
        return jnp.einsum("qbvs,qbsk->qbvk", rows.astype(jnp.float32), factor.astype(jnp.float32))

    state = per_partner(compress_one, own_rows, comp_view)

    other = jnp.take(swap_partner(state, LEVELS - 1), block_map[0], axis=2)
    top_view = top_factor.reshape(n_part, n_blk, LEAVES_DEV, KB, KB)

    def top_one(coeffs, factor):
        return jnp.einsum("qbvk,qbkj->qbvj", coeffs, factor.astype(jnp.float32), precision=HI)

    state = per_partner(top_one, other, top_view)

    for section in range(LEVELS - 1):
        bit = LEVELS - 2 - section
        other = jnp.take(swap_partner(state, bit), block_map[section + 1], axis=2)
        mix_view = butterfly_mixers[section].reshape(n_part, n_blk, LEAVES_DEV, 2, KB, KB)

        def mix_one(own, across_partners, factor):
            widened = factor.astype(jnp.float32)
            first = jnp.einsum("qbvk,qbkj->qbvj", own, widened[:, :, 0], precision=HI)
            second = jnp.einsum("qbvk,qbkj->qbvj", across_partners, widened[:, :, 1], precision=HI)
            return first + second

        state = per_partner(mix_one, state, other, mix_view)

    exp_view = expand.reshape(n_part, n_blk, LEAVES_DEV, KB, LEAF)

    def expand_one(coeffs, factor):
        return jnp.einsum("qbvk,qbks->qbvs", coeffs, factor.astype(jnp.float32), precision=HI)

    far_field = per_partner(expand_one, state, exp_view)
    in_tree = (nearby_field_sum + far_field).astype(jnp.bfloat16)
    in_tree = in_tree.transpose(3, 0, 1, 2, 4).reshape(NV, POINTS)
    applied = jnp.zeros((NV, POINTS), jnp.bfloat16)
    return applied.at[:, tree_order].set(in_tree)
```

```python
import functools

import jax
import jax.numpy as jnp
from jax import lax
from jax.experimental import pallas as pl
from jax.experimental.pallas import tpu as pltpu
from jax.sharding import PartitionSpec as P

BF = jnp.bfloat16
F32 = jnp.float32
MESH = pl.DeviceIdType.MESH
LEAVES = 8
LEAF = 128
NV = 32
SENT = 4


def dot(a, b):
    return jnp.dot(a, b, preferred_element_type=F32)


def halves(x):
    high = x.astype(BF)
    return high, (x - high.astype(F32)).astype(BF)


def stacked(x):
    return jnp.concatenate(halves(x), axis=0)


def paired(w):
    return jnp.concatenate(halves(w), axis=1)


def apply_factor(x, w):
    y = dot(x, w)
    return (y[:NV, :LEAF] + y[NV:, :LEAF]) + y[:NV, LEAF:]


def lane_gather(chunks, where, lane):
    lanes = jnp.broadcast_to(lane, (NV, LEAF))
    chunk_of = jnp.broadcast_to(where, (NV, LEAF))
    out = None
    for k, chunk in enumerate(chunks):
        picked = jnp.take_along_axis(chunk, lanes, axis=1, mode="promise_in_bounds")
        out = picked if out is None else jnp.where(chunk_of == k, picked, out)
    return out


def level_tables(values):
    mask = functools.reduce(lambda a, b: a | b, [jnp.int32(1) << v for v in values])
    chosen = []
    for _ in range(SENT):
        low = mask & (-mask)
        mask = mask ^ low
        chosen.append(sum((low >= (1 << c)).astype(jnp.int32) for c in range(1, LEAVES)))
    places = [sum((c < v).astype(jnp.int32) for c in chosen[:-1]) for v in values]
    return chosen, places


def kernel(
    points, order, near, neighbours, compress, expand, top, mixers, block_map,
    out_ref,
    pts_v, ord_v, near_v, com_v, exp_v, top_v, mix_v, near_s, map_s, tab_s,
    win, field, inv_w, inv_l, acc, out_v,
    snd1, r16, r24, top8_s, top8_r, mix2_s, mix2_r,
    snd2a, snd2b, r4, r6, r2, snd3, r1,
    w1, w2, w3, st2, st4,
    load_sem, ssem, rsem,
):
    p = lax.axis_index("partner")
    b = lax.axis_index("block")
    n_b = lax.axis_size("block")
    me = p * n_b + b
    right = lax.rem(b + 1, n_b)
    left = lax.rem(b + n_b - 1, n_b)

    barrier = pltpu.get_barrier_semaphore()
    for m in (16, 24, 8, 4, 6, 2, 1):
        pl.semaphore_signal(barrier, inc=1, device_id=(p ^ m, b), device_id_type=MESH)
    for z in (left, right):
        pl.semaphore_signal(barrier, inc=1, device_id=(p, z), device_id_type=MESH)

    loads = {}
    for k, (name, src, dst) in enumerate((
        ("map", block_map, map_s), ("order", order, ord_v), ("points", points, pts_v), ("compress", compress, com_v),
        ("top", top, top_v), ("mixers", mixers, mix_v), ("neighbours", neighbours, near_s), ("near", near, near_v),
        ("expand", expand, exp_v),
    )):
        loads[name] = pltpu.make_async_copy(src, dst, load_sem.at[k])
        loads[name].start()

    used = [0]
    sends = []

    def send(src, dst, to):
        k = used[0]
        used[0] += 1
        c = pltpu.make_async_remote_copy(
            src_ref=src, dst_ref=dst, send_sem=ssem.at[k], recv_sem=rsem.at[k], device_id=to, device_id_type=MESH
        )
        c.start()
        sends.append(c)
        return c

    loads["map"].wait()
    chosen, places, entries = [], [], []
    for j in range(5):
        row = [map_s[j, i] for i in range(LEAVES)]
        c, q = level_tables(row)
        chosen.append(c)
        places.append(q)
        entries.append(row)
        for i in range(LEAVES):
            tab_s[j, i] = q[i]

    loads["order"].wait()
    local = ord_v[...] - me * (LEAVES * LEAF)
    ord_v[...] = local
    loads["points"].wait()
    chunks = [pts_v[:, pl.ds(k * LEAF, LEAF)].astype(F32) for k in range(LEAVES)]
    loads["compress"].wait()
    pl.semaphore_wait(barrier, 9)
    first = []
    for s in range(SENT):
        c = chosen[0][s]
        row = ord_v[pl.ds(c, 1), :]
        rows = lane_gather(chunks, row >> 7, row & 127).astype(BF)
        snd1[s] = stacked(dot(rows, com_v[c]))
        first.append(send(snd1.at[s], r16.at[s], (p ^ 16, b)))
        first.append(send(snd1.at[s], r24.at[s], (p ^ 24, b)))

    loads["top"].wait()
    for s in range(SENT):
        top8_s[s] = top_v[chosen[1][s]]
    top_copy = send(top8_s, top8_r, (p ^ 8, b))
    for l in range(LEAVES):
        row = ord_v[pl.ds(l, 1), :]
        win[l + 2] = lane_gather(chunks, row >> 7, row & 127).astype(BF)
    halo_right = send(win.at[pl.ds(LEAVES, 2)], win.at[pl.ds(0, 2)], (p, right))
    halo_left = send(win.at[pl.ds(2, 2)], win.at[pl.ds(LEAVES + 2, 2)], (p, left))
    loads["mixers"].wait()
    for s in range(SENT):
        mix2_s[s] = mix_v[1, chosen[3][s]]
    mix_copy = send(mix2_s, mix2_r, (p ^ 2, b))

    for i in range(LEAVES):
        w1[i, pl.ds(0, LEAF)] = paired(dot(top_v[i], mix_v[0, i, 0]))
    top_copy.wait_recv()
    for i in range(LEAVES):
        w1[i, pl.ds(LEAF, LEAF)] = paired(dot(top8_r[places[1][i]], mix_v[0, i, 1]))

    for c in first:
        c.wait_recv()

    def skeleton_2(c):
        own = r16[tab_s[0, c]]
        other = r24[tab_s[0, map_s[1, c]]]
        return apply_factor(jnp.concatenate([own, other], axis=1), w1[c])

    second = []
    for s in range(SENT):
        snd2a[s] = stacked(skeleton_2(chosen[2][s]))
        second.append(send(snd2a.at[s], r4.at[s], (p ^ 4, b)))
        second.append(send(snd2a.at[s], r6.at[s], (p ^ 6, b)))
    for s in range(SENT):
        snd2b[s] = stacked(skeleton_2(chosen[3][s]))
        second.append(send(snd2b.at[s], r2.at[s], (p ^ 2, b)))
    for i in range(LEAVES):
        st2[i] = stacked(skeleton_2(i))

    for i in range(LEAVES):
        own = mix_v[1, i].reshape(2 * LEAF, LEAF)
        w2[i, pl.ds(0, 2 * LEAF)] = paired(dot(own, mix_v[2, i, 0]))
        acc[i] = apply_factor(st2[i], w2[i, pl.ds(0, LEAF)])
    mix_copy.wait_recv()
    for i in range(LEAVES):
        other = mix2_r[places[3][i]].reshape(2 * LEAF, LEAF)
        w2[i, pl.ds(2 * LEAF, 2 * LEAF)] = paired(dot(other, mix_v[2, i, 1]))
    loads["expand"].wait()
    for i in range(LEAVES):
        w3[i] = paired(dot(mix_v[3, i].reshape(2 * LEAF, LEAF), exp_v[i]))
    loads["near"].wait()
    loads["neighbours"].wait()
    halo_right.wait_recv()
    halo_left.wait_recv()
    for i in range(LEAVES):
        rows = jnp.concatenate([win[jnp.clip(near_s[n, i] - me * LEAVES + 2, 0, LEAVES + 3)] for n in range(3)], axis=1)
        field[i] = dot(rows, near_v[i].reshape(3 * LEAF, LEAF))
    sub = lax.broadcasted_iota(jnp.int32, (LEAVES, LEAF), 0)
    lane = lax.broadcasted_iota(jnp.int32, (LEAVES, LEAF), 1)
    tall = lax.broadcasted_iota(jnp.int32, (LEAF, LEAF), 0)
    table = jnp.zeros((2 * LEAVES, LEAF), F32)
    for l in range(LEAVES):
        row = ord_v[pl.ds(l, 1), :]
        here = jnp.broadcast_to(row >> 7, (LEAVES, LEAF)) == sub
        digits = jnp.concatenate(
            [jnp.where(here, float(l), 0.0), jnp.where(here, lane.astype(F32), 0.0)], axis=0
        ).astype(BF)
        spots = jnp.where(jnp.broadcast_to(row & 127, (LEAF, LEAF)) == tall, 1.0, 0.0).astype(BF)
        table += lax.dot_general(digits, spots, (((1,), (1,)), ((), ())), preferred_element_type=F32)
    inv_w[...] = table[:LEAVES].astype(jnp.int32)
    inv_l[...] = table[LEAVES:].astype(jnp.int32)

    for c in second:
        c.wait_recv()

    def skeleton_4(c):
        x = jnp.concatenate([r4[tab_s[2, c]], r2[tab_s[3, c]], r6[tab_s[2, map_s[3, c]]]], axis=1)
        return acc[c] + apply_factor(x, w2[c, pl.ds(LEAF, 3 * LEAF)])

    third = []
    for s in range(SENT):
        snd3[s] = stacked(skeleton_4(chosen[4][s]))
        third.append(send(snd3.at[s], r1.at[s], (p ^ 1, b)))
    for i in range(LEAVES):
        st4[i] = stacked(skeleton_4(i))
    for i in range(LEAVES):
        field[i] = field[i] + apply_factor(st4[i], w3[i, pl.ds(0, LEAF)])
    for c in third:
        c.wait_recv()
    tree = []
    for i in range(LEAVES):
        tree.append(field[i] + apply_factor(r1[places[4][i]], w3[i, pl.ds(LEAF, LEAF)]))
    for l in range(LEAVES):
        out_v[:, pl.ds(l * LEAF, LEAF)] = lane_gather(tree, inv_w[pl.ds(l, 1), :], inv_l[pl.ds(l, 1), :]).astype(BF)
    done = pltpu.make_async_copy(out_v, out_ref, load_sem.at[9])
    done.start()
    for c in sends:
        c.wait_send()
    done.wait()


def on_device(points, tree_order, near, neighbours, compress, expand, top, mixers, block_map):
    skeleton = pltpu.VMEM((SENT, 2 * NV, LEAF), BF)
    n_copies = 8 + 4 + 12 + 4
    return pl.pallas_call(
        kernel,
        out_shape=jax.ShapeDtypeStruct(points.shape, points.dtype),
        in_specs=[pl.BlockSpec(memory_space=pltpu.HBM)] * 9,
        out_specs=pl.BlockSpec(memory_space=pltpu.HBM),
        scratch_shapes=[
            pltpu.VMEM(points.shape, BF), pltpu.VMEM((LEAVES, LEAF), jnp.int32), pltpu.VMEM(near.shape, BF),
            pltpu.VMEM(compress.shape, BF), pltpu.VMEM(expand.shape, BF), pltpu.VMEM(top.shape, BF),
            pltpu.VMEM(mixers.shape, BF), pltpu.SMEM(neighbours.shape[::-1], jnp.int32), pltpu.SMEM(block_map.shape, jnp.int32),
            pltpu.SMEM(block_map.shape, jnp.int32),
            pltpu.VMEM((LEAVES + 4, NV, LEAF), BF), pltpu.VMEM((LEAVES, NV, LEAF), F32),
            pltpu.VMEM((LEAVES, LEAF), jnp.int32), pltpu.VMEM((LEAVES, LEAF), jnp.int32),
            pltpu.VMEM((LEAVES, NV, LEAF), F32), pltpu.VMEM(points.shape, BF),
            skeleton, skeleton, skeleton,
            pltpu.VMEM((SENT, LEAF, LEAF), BF), pltpu.VMEM((SENT, LEAF, LEAF), BF),
            pltpu.VMEM((SENT, 2, LEAF, LEAF), BF), pltpu.VMEM((SENT, 2, LEAF, LEAF), BF),
            skeleton, skeleton, skeleton, skeleton, skeleton, skeleton, skeleton,
            pltpu.VMEM((LEAVES, 2 * LEAF, 2 * LEAF), BF), pltpu.VMEM((LEAVES, 4 * LEAF, 2 * LEAF), BF),
            pltpu.VMEM((LEAVES, 2 * LEAF, 2 * LEAF), BF),
            pltpu.VMEM((LEAVES, 2 * NV, LEAF), BF), pltpu.VMEM((LEAVES, 2 * NV, LEAF), BF),
            pltpu.SemaphoreType.DMA((10,)), pltpu.SemaphoreType.DMA((n_copies,)), pltpu.SemaphoreType.DMA((n_copies,)),
        ],
        compiler_params=pltpu.CompilerParams(collective_id=0, has_side_effects=True, vmem_limit_bytes=58 * 2**20),
        cost_estimate=pl.CostEstimate(flops=200_000_000, bytes_accessed=4_000_000, transcendentals=0),
        name="butterfly",
    )(points, tree_order.reshape(LEAVES, LEAF), near, neighbours.T, compress, expand, top, mixers, block_map)


def solution(mesh):
    both = ("partner", "block")
    return jax.shard_map(
        on_device,
        mesh=mesh,
        in_specs=(
            P(None, both),
            P(both),
            P(both, None, None, None),
            P(both, None),
            P(both, None, None),
            P(both, None, None),
            P(both, None, None),
            P(None, both, None, None, None),
            P(),
        ),
        out_specs=P(None, both),
        check_vma=False,
    )
```

```python
import functools

import jax
import jax.numpy as jnp
from jax import lax
from jax.experimental import pallas as pl
from jax.experimental.pallas import tpu as pltpu
from jax.sharding import PartitionSpec as P

BF = jnp.bfloat16
F32 = jnp.float32
MESH = pl.DeviceIdType.MESH
LEAVES = 8
LEAF = 128
NV = 32
SENT = 4


def dot(a, b):
    return jnp.dot(a, b, preferred_element_type=F32)


def halves(x):
    high = x.astype(BF)
    return high, (x - high.astype(F32)).astype(BF)


def stacked(x):
    return jnp.concatenate(halves(x), axis=0)


def paired(w):
    return jnp.concatenate(halves(w), axis=1)


def apply_factor(x, w):
    y = dot(x, w)
    return (y[:NV, :LEAF] + y[NV:, :LEAF]) + y[:NV, LEAF:]


def lane_gather(chunks, where, lane):
    lanes = jnp.broadcast_to(lane, (NV, LEAF))
    chunk_of = jnp.broadcast_to(where, (NV, LEAF))
    out = None
    for k, chunk in enumerate(chunks):
        picked = jnp.take_along_axis(chunk, lanes, axis=1, mode="promise_in_bounds")
        out = picked if out is None else jnp.where(chunk_of == k, picked, out)
    return out


def level_tables(values):
    mask = functools.reduce(lambda a, b: a | b, [jnp.int32(1) << v for v in values])
    chosen = []
    for _ in range(SENT):
        low = mask & (-mask)
        mask = mask ^ low
        chosen.append(sum((low >= (1 << c)).astype(jnp.int32) for c in range(1, LEAVES)))
    places = [sum((c < v).astype(jnp.int32) for c in chosen[:-1]) for v in values]
    return chosen, places


def kernel(
    points, order, near, neighbours, compress, expand, top, mixers, block_map,
    out_ref,
    pts_v, ord_v, near_v, com_v, exp_v, top_v, mix_v, near_s, map_s, tab_s,
    win, field, inv_w, inv_l, acc, out_v,
    snd1, r16, r24, top8_s, top8_r, mix2_s, mix2_r,
    snd2a, snd2b, r4, r6, r2, snd3, r1,
    w1, w2, w3, st2, st4,
    load_sem, ssem, rsem, halo_ssem, halo_rsem,
):
    p = lax.axis_index("partner")
    b = lax.axis_index("block")
    n_b = lax.axis_size("block")
    me = p * n_b + b
    has_left, has_right = b > 0, b < n_b - 1
    sides = ((has_left, b - 1), (has_right, b + 1))

    barrier = pltpu.get_barrier_semaphore()
    loads = {}

    def load(k, name, src, dst):
        loads[name] = pltpu.make_async_copy(src, dst, load_sem.at[k])
        loads[name].start()

    partners = (16, 24, 8, 4, 6, 2, 1)
    load(0, "map", block_map, map_s)
    load(1, "order", order, ord_v)
    for m in partners[:3]:
        pl.semaphore_signal(barrier, inc=1, device_id=(p ^ m, b), device_id_type=MESH)
    load(2, "points", points, pts_v)
    load(3, "compress", compress, com_v)
    load(4, "top", top, top_v)
    for m in partners[3:]:
        pl.semaphore_signal(barrier, inc=1, device_id=(p ^ m, b), device_id_type=MESH)
    for there, z in sides:
        @pl.when(there)
        def _():
            pl.semaphore_signal(barrier, inc=1, device_id=(p, z), device_id_type=MESH)
    load(5, "mixers", mixers, mix_v)
    load(6, "expand", expand, exp_v)
    load(7, "near", near, near_v)
    load(8, "neighbours", neighbours, near_s)

    used = [0]
    sends = []

    def send(src, dst, to):
        k = used[0]
        used[0] += 1
        c = pltpu.make_async_remote_copy(
            src_ref=src, dst_ref=dst, send_sem=ssem.at[k], recv_sem=rsem.at[k], device_id=to, device_id_type=MESH
        )
        c.start()
        sends.append(c)
        return c

    loads["map"].wait()
    chosen, places = {}, {}

    def tables(j):
        chosen[j], places[j] = level_tables([map_s[j, i] for i in range(LEAVES)])
        for i in range(LEAVES):
            tab_s[j, i] = places[j][i]

    tables(0)
    tables(1)

    loads["order"].wait()
    loads["points"].wait()
    chunks = [pts_v[:, pl.ds(k * LEAF, LEAF)].astype(F32) for k in range(LEAVES)]
    loads["compress"].wait()
    for s in range(SENT):
        c = chosen[0][s]
        row = ord_v[pl.ds(c, 1), :]
        rows = lane_gather(chunks, (row >> 7) & 7, row & 127).astype(BF)
        snd1[s] = stacked(dot(rows, com_v[c]))
    loads["top"].wait()
    for s in range(SENT):
        top8_s[s] = top_v[chosen[1][s]]

    pl.semaphore_wait(barrier, len(partners) + has_left.astype(jnp.int32) + has_right.astype(jnp.int32))
    first = [send(snd1, r16, (p ^ 16, b)), send(snd1, r24, (p ^ 24, b))]
    top_copy = send(top8_s, top8_r, (p ^ 8, b))
    for j in range(2, 5):
        tables(j)
    for l in range(LEAVES):
        row = ord_v[pl.ds(l, 1), :]
        win[l + 2] = lane_gather(chunks, (row >> 7) & 7, row & 127).astype(BF)
    halo = []
    for k, (there, z, src, dst) in enumerate(((*sides[1], LEAVES, 0), (*sides[0], 2, LEAVES + 2))):
        copy = pltpu.make_async_remote_copy(
            src_ref=win.at[pl.ds(src, 2)], dst_ref=win.at[pl.ds(dst, 2)], send_sem=halo_ssem.at[k],
            recv_sem=halo_rsem.at[k], device_id=(p, z), device_id_type=MESH,
        )
        halo.append((there, sides[k][0], copy, dst))

        @pl.when(there)
        def _():
            copy.start()

        @pl.when(jnp.logical_not(sides[k][0]))
        def _():
            win[dst] = jnp.zeros((NV, LEAF), BF)
            win[dst + 1] = jnp.zeros((NV, LEAF), BF)
    loads["mixers"].wait()
    for s in range(SENT):
        mix2_s[s] = mix_v[1, chosen[3][s]]
    mix_copy = send(mix2_s, mix2_r, (p ^ 2, b))

    for i in range(LEAVES):
        w1[i, pl.ds(0, LEAF)] = paired(dot(top_v[i], mix_v[0, i, 0]))
    for i in range(LEAVES):
        w2[i, pl.ds(0, 2 * LEAF)] = paired(dot(mix_v[1, i].reshape(2 * LEAF, LEAF), mix_v[2, i, 0]))
    loads["expand"].wait()
    for i in range(LEAVES):
        w3[i] = paired(dot(mix_v[3, i].reshape(2 * LEAF, LEAF), exp_v[i]))
    sub = lax.broadcasted_iota(jnp.int32, (LEAVES, LEAF), 0)
    lane = lax.broadcasted_iota(jnp.int32, (LEAVES, LEAF), 1)
    tall = lax.broadcasted_iota(jnp.int32, (LEAF, LEAF), 0)
    table = jnp.zeros((2 * LEAVES, LEAF), F32)
    for l in range(LEAVES):
        row = ord_v[pl.ds(l, 1), :]
        here = jnp.broadcast_to((row >> 7) & 7, (LEAVES, LEAF)) == sub
        digits = jnp.concatenate(
            [jnp.where(here, float(l), 0.0), jnp.where(here, lane.astype(F32), 0.0)], axis=0
        ).astype(BF)
        spots = jnp.where(jnp.broadcast_to(row & 127, (LEAF, LEAF)) == tall, 1.0, 0.0).astype(BF)
        table += lax.dot_general(digits, spots, (((1,), (1,)), ((), ())), preferred_element_type=F32)
    inv_w[...] = table[:LEAVES].astype(jnp.int32)
    inv_l[...] = table[LEAVES:].astype(jnp.int32)

    top_copy.wait_recv()
    for i in range(LEAVES):
        w1[i, pl.ds(LEAF, LEAF)] = paired(dot(top8_r[places[1][i]], mix_v[0, i, 1]))

    for c in first:
        c.wait_recv()

    def skeleton_2(c):
        own = r16[tab_s[0, c]]
        other = r24[tab_s[0, map_s[1, c]]]
        return apply_factor(jnp.concatenate([own, other], axis=1), w1[c])

    for s in range(SENT):
        snd2a[s] = stacked(skeleton_2(chosen[2][s]))
    second = [send(snd2a, r4, (p ^ 4, b)), send(snd2a, r6, (p ^ 6, b))]
    for s in range(SENT):
        snd2b[s] = stacked(skeleton_2(chosen[3][s]))
    second.append(send(snd2b, r2, (p ^ 2, b)))
    for i in range(LEAVES):
        st2[i] = stacked(skeleton_2(i))

    for i in range(LEAVES):
        acc[i] = apply_factor(st2[i], w2[i, pl.ds(0, LEAF)])
    mix_copy.wait_recv()
    for i in range(LEAVES):
        other = mix2_r[places[3][i]].reshape(2 * LEAF, LEAF)
        w2[i, pl.ds(2 * LEAF, 2 * LEAF)] = paired(dot(other, mix_v[2, i, 1]))
    loads["near"].wait()
    loads["neighbours"].wait()
    for _, comes, copy, _ in halo:
        @pl.when(comes)
        def _():
            copy.wait_recv()
    for i in range(LEAVES):
        rows = jnp.concatenate([win[jnp.clip(near_s[n, i] - me * LEAVES + 2, 0, LEAVES + 3)] for n in range(3)], axis=1)
        field[i] = dot(rows, near_v[i].reshape(3 * LEAF, LEAF))
    for c in second:
        c.wait_recv()

    def skeleton_4(c):
        x = jnp.concatenate([r4[tab_s[2, c]], r2[tab_s[3, c]], r6[tab_s[2, map_s[3, c]]]], axis=1)
        return acc[c] + apply_factor(x, w2[c, pl.ds(LEAF, 3 * LEAF)])

    for s in range(SENT):
        snd3[s] = stacked(skeleton_4(chosen[4][s]))
    third = send(snd3, r1, (p ^ 1, b))
    for i in range(LEAVES):
        st4[i] = stacked(skeleton_4(i))
    for i in range(LEAVES):
        field[i] = field[i] + apply_factor(st4[i], w3[i, pl.ds(0, LEAF)])
    third.wait_recv()
    tree = []
    for i in range(LEAVES):
        tree.append(field[i] + apply_factor(r1[places[4][i]], w3[i, pl.ds(LEAF, LEAF)]))
    for l in range(LEAVES):
        out_ref[:, pl.ds(l * LEAF, LEAF)] = lane_gather(tree, inv_w[pl.ds(l, 1), :], inv_l[pl.ds(l, 1), :]).astype(BF)
    for c in sends:
        c.wait_send()
    for there, _, copy, _ in halo:
        @pl.when(there)
        def _():
            copy.wait_send()


def on_device(points, tree_order, near, neighbours, compress, expand, top, mixers, block_map):
    skeleton = pltpu.VMEM((SENT, 2 * NV, LEAF), BF)
    n_copies = 8
    return pl.pallas_call(
        kernel,
        out_shape=pltpu.VMEM(points.shape, points.dtype),
        in_specs=[pl.BlockSpec(memory_space=pltpu.HBM)] * 9,
        out_specs=pl.BlockSpec(memory_space=pltpu.VMEM),
        scratch_shapes=[
            pltpu.VMEM(points.shape, BF), pltpu.VMEM((LEAVES, LEAF), jnp.int32), pltpu.VMEM(near.shape, BF),
            pltpu.VMEM(compress.shape, BF), pltpu.VMEM(expand.shape, BF), pltpu.VMEM(top.shape, BF),
            pltpu.VMEM(mixers.shape, BF), pltpu.SMEM(neighbours.shape[::-1], jnp.int32), pltpu.SMEM(block_map.shape, jnp.int32),
            pltpu.SMEM(block_map.shape, jnp.int32),
            pltpu.VMEM((LEAVES + 4, NV, LEAF), BF), pltpu.VMEM((LEAVES, NV, LEAF), F32),
            pltpu.VMEM((LEAVES, LEAF), jnp.int32), pltpu.VMEM((LEAVES, LEAF), jnp.int32),
            pltpu.VMEM((LEAVES, NV, LEAF), F32), pltpu.VMEM(points.shape, BF),
            skeleton, skeleton, skeleton,
            pltpu.VMEM((SENT, LEAF, LEAF), BF), pltpu.VMEM((SENT, LEAF, LEAF), BF),
            pltpu.VMEM((SENT, 2, LEAF, LEAF), BF), pltpu.VMEM((SENT, 2, LEAF, LEAF), BF),
            skeleton, skeleton, skeleton, skeleton, skeleton, skeleton, skeleton,
            pltpu.VMEM((LEAVES, 2 * LEAF, 2 * LEAF), BF), pltpu.VMEM((LEAVES, 4 * LEAF, 2 * LEAF), BF),
            pltpu.VMEM((LEAVES, 2 * LEAF, 2 * LEAF), BF),
            pltpu.VMEM((LEAVES, 2 * NV, LEAF), BF), pltpu.VMEM((LEAVES, 2 * NV, LEAF), BF),
            pltpu.SemaphoreType.DMA((10,)), pltpu.SemaphoreType.DMA((n_copies,)), pltpu.SemaphoreType.DMA((n_copies,)),
            pltpu.SemaphoreType.DMA((2,)), pltpu.SemaphoreType.DMA((2,)),
        ],
        compiler_params=pltpu.CompilerParams(collective_id=0, has_side_effects=True, vmem_limit_bytes=58 * 2**20),
        cost_estimate=pl.CostEstimate(flops=200_000_000, bytes_accessed=4_000_000, transcendentals=0),
        name="butterfly",
    )(points, tree_order.reshape(LEAVES, LEAF), near, neighbours.T, compress, expand, top, mixers, block_map)


def solution(mesh):
    both = ("partner", "block")
    return jax.shard_map(
        on_device,
        mesh=mesh,
        in_specs=(
            P(None, both),
            P(both),
            P(both, None, None, None),
            P(both, None),
            P(both, None, None),
            P(both, None, None),
            P(both, None, None),
            P(None, both, None, None, None),
            P(),
        ),
        out_specs=P(None, both),
        check_vma=False,
    )
```

```python
import functools

import jax
import jax.numpy as jnp
from jax import lax
from jax.experimental import pallas as pl
from jax.experimental.pallas import tpu as pltpu
from jax.sharding import PartitionSpec as P

BF = jnp.bfloat16
F32 = jnp.float32
MESH = pl.DeviceIdType.MESH
LEAVES = 8
LEAF = 128
NV = 32
SENT = 4


def dot(a, b):
    return jnp.dot(a, b, preferred_element_type=F32)


def halves(x):
    high = x.astype(BF)
    return high, (x - high.astype(F32)).astype(BF)


def stacked(x):
    return jnp.concatenate(halves(x), axis=0)


def paired(w):
    return jnp.concatenate(halves(w), axis=1)


def apply_factor(x, w):
    y = dot(x, w)
    return (y[:NV, :LEAF] + y[NV:, :LEAF]) + y[:NV, LEAF:]


def apply_exact(x, w):
    y = dot(x, w)
    return y[:NV] + y[NV:]


def lane_gather(chunks, where, lane):
    lanes = jnp.broadcast_to(lane, (NV, LEAF))
    chunk_of = jnp.broadcast_to(where, (NV, LEAF))
    out = None
    for k, chunk in enumerate(chunks):
        picked = jnp.take_along_axis(chunk, lanes, axis=1, mode="promise_in_bounds")
        out = picked if out is None else jnp.where(chunk_of == k, picked, out)
    return out


def level_tables(values):
    mask = functools.reduce(lambda a, b: a | b, [jnp.int32(1) << v for v in values])
    chosen = []
    for _ in range(SENT):
        low = mask & (-mask)
        mask = mask ^ low
        chosen.append(sum((low >= (1 << c)).astype(jnp.int32) for c in range(1, LEAVES)))
    places = [sum((c < v).astype(jnp.int32) for c in chosen[:-1]) for v in values]
    return chosen, places


def kernel(
    points, order, near, neighbours, compress, expand, top, mixers, block_map,
    out_ref,
    pts_v, ord_v, near_v, com_v, exp_v, top_v, mix_v, near_s, map_s, tab_s,
    win, field, inv_w, inv_l, acc, out_v,
    snd1, r16, r24, top8_s, top8_r, mix2_s, mix2_r,
    snd2a, snd2b, r4, r6, r2, snd3, r1,
    w1, w2, w3, st2, st4, own1, part,
    load_sem, ssem, rsem, halo_ssem, halo_rsem, entered,
):
    p = lax.axis_index("partner")
    b = lax.axis_index("block")
    n_b = lax.axis_size("block")
    me = p * n_b + b
    has_left, has_right = b > 0, b < n_b - 1

    barrier = pltpu.get_barrier_semaphore()
    loads = {}

    def load(k, name, src, dst):
        loads[name] = pltpu.make_async_copy(src, dst, load_sem.at[k])
        loads[name].start()

    load(0, "map", block_map, map_s)
    load(1, "order", order, ord_v)
    for m in (16, 24, 8):
        pl.semaphore_signal(barrier, inc=1, device_id=(p ^ m, b), device_id_type=MESH)
    load(2, "points", points, pts_v)
    load(3, "compress", compress, com_v)
    load(4, "top", top, top_v)
    late = (4, 6, 2, 1)
    waits = [((p >> bit) & 1 == 1) != (p < 8) for bit in (2, 2, 1, 0)]
    for m, waiter in zip(late, waits):
        @pl.when(jnp.logical_not(waiter))
        def _():
            pl.semaphore_signal(barrier, inc=1, device_id=(p ^ m, b), device_id_type=MESH)

    @pl.when(has_right)
    def _():
        pl.semaphore_signal(barrier, inc=1, device_id=(p, b + 1), device_id_type=MESH)
    load(5, "mixers", mixers, mix_v)
    load(6, "expand", expand, exp_v)
    load(7, "near", near, near_v)
    load(8, "neighbours", neighbours, near_s)

    used = [0]
    sends = []

    def send(src, dst, to):
        k = used[0]
        used[0] += 1
        c = pltpu.make_async_remote_copy(
            src_ref=src, dst_ref=dst, send_sem=ssem.at[k], recv_sem=rsem.at[k], device_id=to, device_id_type=MESH
        )
        c.start()
        sends.append(c)
        return c

    loads["map"].wait()
    chosen, places = {}, {}

    def tables(j):
        chosen[j], places[j] = level_tables([map_s[j, i] for i in range(LEAVES)])
        for i in range(LEAVES):
            tab_s[j, i] = places[j][i]

    tables(0)
    tables(1)

    loads["order"].wait()
    loads["points"].wait()
    chunks = [pts_v[:, pl.ds(k * LEAF, LEAF)].astype(F32) for k in range(LEAVES)]
    loads["compress"].wait()
    for s in range(SENT):
        c = chosen[0][s]
        row = ord_v[pl.ds(c, 1), :]
        rows = lane_gather(chunks, (row >> 7) & 7, row & 127).astype(BF)
        snd1[s] = stacked(dot(rows, com_v[c]))
    loads["top"].wait()
    for s in range(SENT):
        top8_s[s] = top_v[chosen[1][s]]

    pl.semaphore_wait(barrier, 3 + sum(w.astype(jnp.int32) for w in (has_left, *waits)))
    first = [send(snd1, r16, (p ^ 16, b)), send(snd1, r24, (p ^ 24, b))]
    top_copy = send(top8_s, top8_r, (p ^ 8, b))
    for k, (m, waiter) in enumerate(zip(late, waits)):
        @pl.when(waiter)
        def _():
            pl.semaphore_signal(entered.at[k], inc=1, device_id=(p ^ m, b), device_id_type=MESH)

    def meet(k):
        @pl.when(jnp.logical_not(waits[k]))
        def _():
            pl.semaphore_wait(entered.at[k], 1)

    for j in range(2, 5):
        tables(j)
    for l in range(LEAVES):
        row = ord_v[pl.ds(l, 1), :]
        win[l + 2] = lane_gather(chunks, (row >> 7) & 7, row & 127).astype(BF)
    to_left = pltpu.make_async_remote_copy(
        src_ref=win.at[pl.ds(2, 2)], dst_ref=win.at[pl.ds(LEAVES + 2, 2)], send_sem=halo_ssem.at[0],
        recv_sem=halo_rsem.at[0], device_id=(p, b - 1), device_id_type=MESH,
    )
    to_right = pltpu.make_async_remote_copy(
        src_ref=win.at[pl.ds(LEAVES, 2)], dst_ref=win.at[pl.ds(0, 2)], send_sem=halo_ssem.at[1],
        recv_sem=halo_rsem.at[1], device_id=(p, b + 1), device_id_type=MESH,
    )

    @pl.when(has_left)
    def _():
        pl.semaphore_signal(entered.at[4], inc=1, device_id=(p, b - 1), device_id_type=MESH)
        to_left.start()

    @pl.when(jnp.logical_not(has_left))
    def _():
        win[0] = jnp.zeros((NV, LEAF), BF)
        win[1] = jnp.zeros((NV, LEAF), BF)

    @pl.when(jnp.logical_not(has_right))
    def _():
        win[LEAVES + 2] = jnp.zeros((NV, LEAF), BF)
        win[LEAVES + 3] = jnp.zeros((NV, LEAF), BF)
    loads["mixers"].wait()
    for s in range(SENT):
        mix2_s[s] = mix_v[1, chosen[3][s], 1]

    for i in range(LEAVES):
        w1[i] = paired(dot(top_v[i], mix_v[0, i, 0]))
    for i in range(LEAVES):
        w2[i, pl.ds(0, 2 * LEAF)] = paired(dot(mix_v[1, i].reshape(2 * LEAF, LEAF), mix_v[2, i, 0]))
    loads["expand"].wait()
    for i in range(LEAVES):
        w3[i] = paired(dot(mix_v[3, i].reshape(2 * LEAF, LEAF), exp_v[i]))
    sub = lax.broadcasted_iota(jnp.int32, (LEAVES, LEAF), 0)
    lane = lax.broadcasted_iota(jnp.int32, (LEAVES, LEAF), 1)
    tall = lax.broadcasted_iota(jnp.int32, (LEAF, LEAF), 0)
    table = jnp.zeros((2 * LEAVES, LEAF), F32)
    for l in range(LEAVES):
        row = ord_v[pl.ds(l, 1), :]
        here = jnp.broadcast_to((row >> 7) & 7, (LEAVES, LEAF)) == sub
        digits = jnp.concatenate(
            [jnp.where(here, float(l), 0.0), jnp.where(here, lane.astype(F32), 0.0)], axis=0
        ).astype(BF)
        spots = jnp.where(jnp.broadcast_to(row & 127, (LEAF, LEAF)) == tall, 1.0, 0.0).astype(BF)
        table += lax.dot_general(digits, spots, (((1,), (1,)), ((), ())), preferred_element_type=F32)
    inv_w[...] = table[:LEAVES].astype(jnp.int32)
    inv_l[...] = table[LEAVES:].astype(jnp.int32)

    meet(2)
    mix_copy = send(mix2_s, mix2_r, (p ^ 2, b))
    for c in first:
        c.wait_recv()
    for i in range(LEAVES):
        own1[i] = apply_factor(r16[places[0][i]], w1[i])
    top_copy.wait_recv()
    for s in range(SENT):
        part[s] = stacked(apply_exact(r24[tab_s[0, chosen[1][s]]], top8_r[s]))

    def skeleton_2(c):
        return own1[c] + apply_exact(part[tab_s[1, c]], mix_v[0, c, 1])

    for s in range(SENT):
        snd2a[s] = stacked(skeleton_2(chosen[2][s]))
    meet(0)
    meet(1)
    second = [send(snd2a, r4, (p ^ 4, b)), send(snd2a, r6, (p ^ 6, b))]
    for s in range(SENT):
        c = chosen[3][s]
        snd2b[s] = stacked(apply_exact(stacked(skeleton_2(c)), mix_v[1, c, 0]))
    second.append(send(snd2b, r2, (p ^ 2, b)))
    @pl.when(has_right)
    def _():
        pl.semaphore_wait(entered.at[4], 1)
        to_right.start()

    for i in range(LEAVES):
        st2[i] = stacked(skeleton_2(i))

    for i in range(LEAVES):
        acc[i] = apply_factor(st2[i], w2[i, pl.ds(0, LEAF)])
    mix_copy.wait_recv()
    for i in range(LEAVES):
        w2[i, pl.ds(2 * LEAF, LEAF)] = paired(dot(mix2_r[places[3][i]], mix_v[2, i, 1]))
    loads["near"].wait()
    loads["neighbours"].wait()
    @pl.when(has_left)
    def _():
        to_right.wait_recv()

    @pl.when(has_right)
    def _():
        to_left.wait_recv()

    for i in range(LEAVES):
        rows = jnp.concatenate([win[jnp.clip(near_s[n, i] - me * LEAVES + 2, 0, LEAVES + 3)] for n in range(3)], axis=1)
        field[i] = dot(rows, near_v[i].reshape(3 * LEAF, LEAF))
    for c in second:
        c.wait_recv()

    def skeleton_4(c):
        x = jnp.concatenate([r4[tab_s[2, c]], r6[tab_s[2, map_s[3, c]]]], axis=1)
        y = acc[c] + apply_exact(r2[tab_s[3, c]], mix_v[2, c, 1])
        return y + apply_factor(x, w2[c, pl.ds(LEAF, 2 * LEAF)])

    for s in range(SENT):
        snd3[s] = stacked(skeleton_4(chosen[4][s]))
    meet(3)
    third = send(snd3, r1, (p ^ 1, b))
    for i in range(LEAVES):
        st4[i] = stacked(skeleton_4(i))
    for i in range(LEAVES):
        field[i] = field[i] + apply_factor(st4[i], w3[i, pl.ds(0, LEAF)])
    third.wait_recv()
    tree = []
    for i in range(LEAVES):
        tree.append(field[i] + apply_factor(r1[places[4][i]], w3[i, pl.ds(LEAF, LEAF)]))
    for l in range(LEAVES):
        out_ref[:, pl.ds(l * LEAF, LEAF)] = lane_gather(tree, inv_w[pl.ds(l, 1), :], inv_l[pl.ds(l, 1), :]).astype(BF)
    for c in sends:
        c.wait_send()
    @pl.when(has_left)
    def _():
        to_left.wait_send()

    @pl.when(has_right)
    def _():
        to_right.wait_send()


def on_device(points, tree_order, near, neighbours, compress, expand, top, mixers, block_map):
    skeleton = pltpu.VMEM((SENT, 2 * NV, LEAF), BF)
    n_copies = 8
    return pl.pallas_call(
        kernel,
        out_shape=pltpu.VMEM(points.shape, points.dtype),
        in_specs=[pl.BlockSpec(memory_space=pltpu.HBM)] * 9,
        out_specs=pl.BlockSpec(memory_space=pltpu.VMEM),
        scratch_shapes=[
            pltpu.VMEM(points.shape, BF), pltpu.VMEM((LEAVES, LEAF), jnp.int32), pltpu.VMEM(near.shape, BF),
            pltpu.VMEM(compress.shape, BF), pltpu.VMEM(expand.shape, BF), pltpu.VMEM(top.shape, BF),
            pltpu.VMEM(mixers.shape, BF), pltpu.SMEM(neighbours.shape[::-1], jnp.int32), pltpu.SMEM(block_map.shape, jnp.int32),
            pltpu.SMEM(block_map.shape, jnp.int32),
            pltpu.VMEM((LEAVES + 4, NV, LEAF), BF), pltpu.VMEM((LEAVES, NV, LEAF), F32),
            pltpu.VMEM((LEAVES, LEAF), jnp.int32), pltpu.VMEM((LEAVES, LEAF), jnp.int32),
            pltpu.VMEM((LEAVES, NV, LEAF), F32), pltpu.VMEM(points.shape, BF),
            skeleton, skeleton, skeleton,
            pltpu.VMEM((SENT, LEAF, LEAF), BF), pltpu.VMEM((SENT, LEAF, LEAF), BF),
            pltpu.VMEM((SENT, LEAF, LEAF), BF), pltpu.VMEM((SENT, LEAF, LEAF), BF),
            skeleton, skeleton, skeleton, skeleton, skeleton, skeleton, skeleton,
            pltpu.VMEM((LEAVES, LEAF, 2 * LEAF), BF), pltpu.VMEM((LEAVES, 3 * LEAF, 2 * LEAF), BF),
            pltpu.VMEM((LEAVES, 2 * LEAF, 2 * LEAF), BF),
            pltpu.VMEM((LEAVES, 2 * NV, LEAF), BF), pltpu.VMEM((LEAVES, 2 * NV, LEAF), BF),
            pltpu.VMEM((LEAVES, NV, LEAF), F32), skeleton,
            pltpu.SemaphoreType.DMA((9,)), pltpu.SemaphoreType.DMA((n_copies,)), pltpu.SemaphoreType.DMA((n_copies,)),
            pltpu.SemaphoreType.DMA((2,)), pltpu.SemaphoreType.DMA((2,)), pltpu.SemaphoreType.REGULAR((5,)),
        ],
        compiler_params=pltpu.CompilerParams(collective_id=0, has_side_effects=True, vmem_limit_bytes=58 * 2**20),
        cost_estimate=pl.CostEstimate(flops=200_000_000, bytes_accessed=4_000_000, transcendentals=0),
        name="butterfly",
    )(points, tree_order.reshape(LEAVES, LEAF), near, neighbours.T, compress, expand, top, mixers, block_map)


def solution(mesh):
    both = ("partner", "block")
    return jax.shard_map(
        on_device,
        mesh=mesh,
        in_specs=(
            P(None, both),
            P(both),
            P(both, None, None, None),
            P(both, None),
            P(both, None, None),
            P(both, None, None),
            P(both, None, None),
            P(None, both, None, None, None),
            P(),
        ),
        out_specs=P(None, both),
        check_vma=False,
    )
```

```python
import functools

import jax
import jax.numpy as jnp
from jax import lax
from jax.experimental import pallas as pl
from jax.experimental.pallas import tpu as pltpu
from jax.sharding import PartitionSpec as P

BF = jnp.bfloat16
F32 = jnp.float32
MESH = pl.DeviceIdType.MESH
LEAVES = 8
LEAF = 128
NV = 32
SENT = 4


def dot(a, b):
    return jnp.dot(a, b, preferred_element_type=F32)


def halves(x):
    high = x.astype(BF)
    return high, (x - high.astype(F32)).astype(BF)


def stacked(x):
    return jnp.concatenate(halves(x), axis=0)


def paired(w):
    return jnp.concatenate(halves(w), axis=1)


def apply_factor(x, w):
    y = dot(x, w)
    return (y[:NV, :LEAF] + y[NV:, :LEAF]) + y[:NV, LEAF:]


def apply_exact(x, w):
    y = dot(x, w)
    return y[:NV] + y[NV:]


def lane_gather(chunks, where, lane):
    lanes = jnp.broadcast_to(lane, (NV, LEAF))
    chunk_of = jnp.broadcast_to(where, (NV, LEAF))
    out = None
    for k, chunk in enumerate(chunks):
        picked = jnp.take_along_axis(chunk, lanes, axis=1, mode="promise_in_bounds")
        out = picked if out is None else jnp.where(chunk_of == k, picked, out)
    return out


def level_tables(values):
    mask = functools.reduce(lambda a, b: a | b, [jnp.int32(1) << v for v in values])
    chosen = []
    for _ in range(SENT):
        low = mask & (-mask)
        mask = mask ^ low
        chosen.append(sum((low >= (1 << c)).astype(jnp.int32) for c in range(1, LEAVES)))
    places = [sum((c < v).astype(jnp.int32) for c in chosen[:-1]) for v in values]
    return chosen, places


def kernel(
    points, order, near, neighbours, compress, expand, top, mixers, block_map,
    out_ref,
    pts_v, ord_v, near_v, com_v, exp_v, top_v, mix_v, near_s, map_s, tab_s,
    win, field, inv_w, inv_l, acc,
    snd1, rec1, top8_s, top8_r, mix2_s, mix2_r,
    snd2a, snd2b, rec2, snd3, r1,
    w1, w2, w3, st2, st4, own1, part,
    load_sem, ssem, rsem, halo_ssem, halo_rsem, entered,
):
    p = lax.axis_index("partner")
    b = lax.axis_index("block")
    n_b = lax.axis_size("block")
    me = p * n_b + b
    has_left, has_right = b > 0, b < n_b - 1

    barrier = pltpu.get_barrier_semaphore()
    loads = {}

    def load(k, name, src, dst):
        loads[name] = pltpu.make_async_copy(src, dst, load_sem.at[k])
        loads[name].start()

    def arrived(part, sem):
        pltpu.make_async_copy(part, part, sem).wait()

    load(0, "map", block_map, map_s)
    load(1, "order", order, ord_v)
    for m in (16, 24, 8):
        pl.semaphore_signal(barrier, inc=1, device_id=(p ^ m, b), device_id_type=MESH)
    load(2, "points", points, pts_v)
    load(2, "compress", compress, com_v)
    load(2, "top", top, top_v)
    late = (4, 6, 2, 1)
    waits = [((p >> bit) & 1 == 1) != (p < 8) for bit in (2, 2, 1, 0)]
    for m, waiter in zip(late, waits):
        @pl.when(jnp.logical_not(waiter))
        def _():
            pl.semaphore_signal(barrier, inc=1, device_id=(p ^ m, b), device_id_type=MESH)

    @pl.when(has_right)
    def _():
        pl.semaphore_signal(barrier, inc=1, device_id=(p, b + 1), device_id_type=MESH)
    load(3, "mixers", mixers, mix_v)
    load(4, "expand", expand, exp_v)
    load(4, "near", near, near_v)
    load(5, "neighbours", neighbours, near_s)


    def send(k, src, dst, to):
        c = pltpu.make_async_remote_copy(
            src_ref=src, dst_ref=dst, send_sem=ssem.at[0], recv_sem=rsem.at[k], device_id=to, device_id_type=MESH
        )
        c.start()
        return c

    loads["map"].wait()
    chosen, places = {}, {}

    def tables(j):
        chosen[j], places[j] = level_tables([map_s[j, i] for i in range(LEAVES)])
        for i in range(LEAVES):
            tab_s[j, i] = places[j][i]

    tables(0)

    loads["order"].wait()
    arrived(mix_v.at[pl.ds(0, 3), pl.ds(0, 3)], load_sem.at[2])
    chunks = [pts_v[:, pl.ds(k * LEAF, LEAF)].astype(F32) for k in range(LEAVES)]
    for s in range(SENT):
        c = chosen[0][s]
        row = ord_v[pl.ds(c, 1), :]
        rows = lane_gather(chunks, (row >> 7) & 7, row & 127).astype(BF)
        snd1[s] = stacked(dot(rows, com_v[c]))
    pl.semaphore_wait(barrier, 3 + sum(w.astype(jnp.int32) for w in (has_left, *waits)))
    send(0, snd1, rec1.at[1], (p ^ 24, b))
    send(0, snd1, rec1.at[0], (p ^ 16, b))
    tables(1)
    for s in range(SENT):
        top8_s[s] = top_v[chosen[1][s]]
    top_copy = send(1, top8_s, top8_r, (p ^ 8, b))
    for k, (m, waiter) in enumerate(zip(late, waits)):
        @pl.when(waiter)
        def _():
            pl.semaphore_signal(entered.at[k], inc=1, device_id=(p ^ m, b), device_id_type=MESH)

    def meet(k):
        @pl.when(jnp.logical_not(waits[k]))
        def _():
            pl.semaphore_wait(entered.at[k], 1)

    for j in range(2, 5):
        tables(j)
    for l in range(LEAVES):
        row = ord_v[pl.ds(l, 1), :]
        win[l + 2] = lane_gather(chunks, (row >> 7) & 7, row & 127).astype(BF)
    to_left = pltpu.make_async_remote_copy(
        src_ref=win.at[pl.ds(2, 2)], dst_ref=win.at[pl.ds(LEAVES + 2, 2)], send_sem=halo_ssem.at[0],
        recv_sem=halo_rsem.at[0], device_id=(p, b - 1), device_id_type=MESH,
    )
    to_right = pltpu.make_async_remote_copy(
        src_ref=win.at[pl.ds(LEAVES, 2)], dst_ref=win.at[pl.ds(0, 2)], send_sem=halo_ssem.at[1],
        recv_sem=halo_rsem.at[1], device_id=(p, b + 1), device_id_type=MESH,
    )

    @pl.when(has_left)
    def _():
        pl.semaphore_signal(entered.at[4], inc=1, device_id=(p, b - 1), device_id_type=MESH)
        to_left.start()

    @pl.when(jnp.logical_not(has_left))
    def _():
        win[0] = jnp.zeros((NV, LEAF), BF)
        win[1] = jnp.zeros((NV, LEAF), BF)

    @pl.when(jnp.logical_not(has_right))
    def _():
        win[LEAVES + 2] = jnp.zeros((NV, LEAF), BF)
        win[LEAVES + 3] = jnp.zeros((NV, LEAF), BF)
    loads["mixers"].wait()
    for s in range(SENT):
        mix2_s[s] = mix_v[1, chosen[3][s], 1]

    for i in range(LEAVES):
        w1[i] = paired(dot(top_v[i], mix_v[0, i, 0]))
    for i in range(LEAVES):
        w2[i, pl.ds(0, 2 * LEAF)] = paired(dot(mix_v[1, i].reshape(2 * LEAF, LEAF), mix_v[2, i, 0]))
    arrived(mix_v.at[pl.ds(0, 2)], load_sem.at[4])
    for i in range(LEAVES):
        w3[i] = paired(dot(mix_v[3, i].reshape(2 * LEAF, LEAF), exp_v[i]))
    sub = lax.broadcasted_iota(jnp.int32, (LEAVES, LEAF), 0)
    lane = lax.broadcasted_iota(jnp.int32, (LEAVES, LEAF), 1)
    tall = lax.broadcasted_iota(jnp.int32, (LEAF, LEAF), 0)
    table = jnp.zeros((2 * LEAVES, LEAF), F32)
    for l in range(LEAVES):
        row = ord_v[pl.ds(l, 1), :]
        here = jnp.broadcast_to((row >> 7) & 7, (LEAVES, LEAF)) == sub
        digits = jnp.concatenate(
            [jnp.where(here, float(l), 0.0), jnp.where(here, lane.astype(F32), 0.0)], axis=0
        ).astype(BF)
        spots = jnp.where(jnp.broadcast_to(row & 127, (LEAF, LEAF)) == tall, 1.0, 0.0).astype(BF)
        table += lax.dot_general(digits, spots, (((1,), (1,)), ((), ())), preferred_element_type=F32)
    inv_w[...] = table[:LEAVES].astype(jnp.int32)
    inv_l[...] = table[LEAVES:].astype(jnp.int32)

    meet(2)
    mix_copy = send(2, mix2_s, mix2_r, (p ^ 2, b))
    arrived(rec1, rsem.at[0])
    for i in range(LEAVES):
        own1[i] = apply_factor(rec1[0, places[0][i]], w1[i])
    top_copy.wait_recv()
    for s in range(SENT):
        part[s] = stacked(apply_exact(rec1[1, tab_s[0, chosen[1][s]]], top8_r[s]))

    def skeleton_2(c):
        return own1[c] + apply_exact(part[tab_s[1, c]], mix_v[0, c, 1])

    for s in range(SENT):
        snd2a[s] = stacked(skeleton_2(chosen[2][s]))
    meet(0)
    meet(1)
    send(3, snd2a, rec2.at[1], (p ^ 6, b))
    send(3, snd2a, rec2.at[0], (p ^ 4, b))
    for s in range(SENT):
        c = chosen[3][s]
        snd2b[s] = stacked(apply_exact(stacked(skeleton_2(c)), mix_v[1, c, 0]))
    send(3, snd2b, rec2.at[2], (p ^ 2, b))
    @pl.when(has_right)
    def _():
        pl.semaphore_wait(entered.at[4], 1)
        to_right.start()

    for i in range(LEAVES):
        st2[i] = stacked(skeleton_2(i))

    for i in range(LEAVES):
        acc[i] = apply_factor(st2[i], w2[i, pl.ds(0, LEAF)])
    mix_copy.wait_recv()
    for i in range(LEAVES):
        w2[i, pl.ds(2 * LEAF, LEAF)] = paired(dot(mix2_r[places[3][i]], mix_v[2, i, 1]))
    loads["neighbours"].wait()
    @pl.when(has_left)
    def _():
        to_right.wait_recv()

    @pl.when(has_right)
    def _():
        to_left.wait_recv()

    for i in range(LEAVES):
        rows = jnp.concatenate([win[jnp.clip(near_s[n, i] - me * LEAVES + 2, 0, LEAVES + 3)] for n in range(3)], axis=1)
        field[i] = dot(rows, near_v[i].reshape(3 * LEAF, LEAF))
    arrived(rec2, rsem.at[3])

    def skeleton_4(c):
        x = jnp.concatenate([rec2[0, tab_s[2, c]], rec2[1, tab_s[2, map_s[3, c]]]], axis=1)
        y = acc[c] + apply_exact(rec2[2, tab_s[3, c]], mix_v[2, c, 1])
        return y + apply_factor(x, w2[c, pl.ds(LEAF, 2 * LEAF)])

    for s in range(SENT):
        snd3[s] = stacked(skeleton_4(chosen[4][s]))
    meet(3)
    third = send(4, snd3, r1, (p ^ 1, b))
    for i in range(LEAVES):
        st4[i] = stacked(skeleton_4(i))
    for i in range(LEAVES):
        field[i] = field[i] + apply_factor(st4[i], w3[i, pl.ds(0, LEAF)])
    third.wait_recv()
    tree = []
    for i in range(LEAVES):
        tree.append(field[i] + apply_factor(r1[places[4][i]], w3[i, pl.ds(LEAF, LEAF)]))
    for l in range(LEAVES):
        out_ref[:, pl.ds(l * LEAF, LEAF)] = lane_gather(tree, inv_w[pl.ds(l, 1), :], inv_l[pl.ds(l, 1), :]).astype(BF)
    arrived(mix_v.at[pl.ds(0, 2), pl.ds(0, 5)], ssem.at[0])
    @pl.when(has_left)
    def _():
        to_left.wait_send()

    @pl.when(has_right)
    def _():
        to_right.wait_send()


def on_device(points, tree_order, near, neighbours, compress, expand, top, mixers, block_map):
    skeleton = pltpu.VMEM((SENT, 2 * NV, LEAF), BF)

    def received(count):
        return pltpu.VMEM((count, SENT, 2 * NV, LEAF), BF)

    return pl.pallas_call(
        kernel,
        out_shape=pltpu.VMEM(points.shape, points.dtype),
        in_specs=[pl.BlockSpec(memory_space=pltpu.HBM)] * 9,
        out_specs=pl.BlockSpec(memory_space=pltpu.VMEM),
        scratch_shapes=[
            pltpu.VMEM(points.shape, BF), pltpu.VMEM((LEAVES, LEAF), jnp.int32), pltpu.VMEM(near.shape, BF),
            pltpu.VMEM(compress.shape, BF), pltpu.VMEM(expand.shape, BF), pltpu.VMEM(top.shape, BF),
            pltpu.VMEM(mixers.shape, BF), pltpu.SMEM(neighbours.shape[::-1], jnp.int32), pltpu.SMEM(block_map.shape, jnp.int32),
            pltpu.SMEM(block_map.shape, jnp.int32),
            pltpu.VMEM((LEAVES + 4, NV, LEAF), BF), pltpu.VMEM((LEAVES, NV, LEAF), F32),
            pltpu.VMEM((LEAVES, LEAF), jnp.int32), pltpu.VMEM((LEAVES, LEAF), jnp.int32),
            pltpu.VMEM((LEAVES, NV, LEAF), F32),
            skeleton, received(2),
            pltpu.VMEM((SENT, LEAF, LEAF), BF), pltpu.VMEM((SENT, LEAF, LEAF), BF),
            pltpu.VMEM((SENT, LEAF, LEAF), BF), pltpu.VMEM((SENT, LEAF, LEAF), BF),
            skeleton, skeleton, received(3), skeleton, skeleton,
            pltpu.VMEM((LEAVES, LEAF, 2 * LEAF), BF), pltpu.VMEM((LEAVES, 3 * LEAF, 2 * LEAF), BF),
            pltpu.VMEM((LEAVES, 2 * LEAF, 2 * LEAF), BF),
            pltpu.VMEM((LEAVES, 2 * NV, LEAF), BF), pltpu.VMEM((LEAVES, 2 * NV, LEAF), BF),
            pltpu.VMEM((LEAVES, NV, LEAF), F32), skeleton,
            pltpu.SemaphoreType.DMA((6,)), pltpu.SemaphoreType.DMA((1,)), pltpu.SemaphoreType.DMA((5,)),
            pltpu.SemaphoreType.DMA((2,)), pltpu.SemaphoreType.DMA((2,)), pltpu.SemaphoreType.REGULAR((5,)),
        ],
        compiler_params=pltpu.CompilerParams(collective_id=0, has_side_effects=True, vmem_limit_bytes=58 * 2**20),
        cost_estimate=pl.CostEstimate(flops=200_000_000, bytes_accessed=4_000_000, transcendentals=0),
        name="butterfly",
    )(points, tree_order.reshape(LEAVES, LEAF), near, neighbours.T, compress, expand, top, mixers, block_map)


def solution(mesh):
    both = ("partner", "block")
    return jax.shard_map(
        on_device,
        mesh=mesh,
        in_specs=(
            P(None, both),
            P(both),
            P(both, None, None, None),
            P(both, None),
            P(both, None, None),
            P(both, None, None),
            P(both, None, None),
            P(None, both, None, None, None),
            P(),
        ),
        out_specs=P(None, both),
        check_vma=False,
    )
```

```python
import functools

import jax
import jax.numpy as jnp
from jax import lax
from jax.experimental import pallas as pl
from jax.experimental.pallas import tpu as pltpu
from jax.sharding import PartitionSpec as P

BF = jnp.bfloat16
F32 = jnp.float32
MESH = pl.DeviceIdType.MESH
LEAVES = 8
LEAF = 128
NV = 32
SENT = 4


def dot(a, b):
    return jnp.dot(a, b, preferred_element_type=F32)


def halves(x):
    high = x.astype(BF)
    return high, (x - high.astype(F32)).astype(BF)


def stacked(x):
    return jnp.concatenate(halves(x), axis=0)


def paired(w):
    return jnp.concatenate(halves(w), axis=1)


def apply_factor(x, w):
    y = dot(x, w)
    return (y[:NV, :LEAF] + y[NV:, :LEAF]) + y[:NV, LEAF:]


def apply_exact(x, w):
    y = dot(x, w)
    return y[:NV] + y[NV:]


def lane_gather(chunks, where, lane):
    lanes = jnp.broadcast_to(lane, (NV, LEAF))
    chunk_of = jnp.broadcast_to(where, (NV, LEAF))
    out = None
    for k, chunk in enumerate(chunks):
        picked = jnp.take_along_axis(chunk, lanes, axis=1, mode="promise_in_bounds")
        out = picked if out is None else jnp.where(chunk_of == k, picked, out)
    return out


def level_tables(values):
    mask = functools.reduce(lambda a, b: a | b, [jnp.int32(1) << v for v in values])
    chosen = []
    for _ in range(SENT):
        low = mask & (-mask)
        mask = mask ^ low
        chosen.append(sum((low >= (1 << c)).astype(jnp.int32) for c in range(1, LEAVES)))
    places = [sum((c < v).astype(jnp.int32) for c in chosen[:-1]) for v in values]
    return chosen, places


def kernel(
    points, order, near, neighbours, compress, expand, top, mixers, block_map,
    out_ref,
    pts_v, ord_v, near_v, com_v, exp_v, top_v, mix_v, near_s, map_s, tab_s,
    win, field, inv_w, inv_l, acc,
    snd1, rec1, top8_s, top8_r, mix2_s, mix2_r,
    snd2a, snd2b, rec2, snd3, r1,
    w1, w2, w3, st2, st4, own1, part,
    load_sem, ssem, rsem, halo_ssem, halo_rsem, entered,
):
    p = lax.axis_index("partner")
    b = lax.axis_index("block")
    n_b = lax.axis_size("block")
    me = p * n_b + b
    has_left, has_right = b > 0, b < n_b - 1

    barrier = pltpu.get_barrier_semaphore()
    loads = {}

    def load(k, name, src, dst):
        loads[name] = pltpu.make_async_copy(src, dst, load_sem.at[k])
        loads[name].start()

    def arrived(part, sem):
        pltpu.make_async_copy(part, part, sem).wait()

    load(0, "map", block_map, map_s)
    load(1, "order", order, ord_v)
    for m in (16, 24, 8):
        pl.semaphore_signal(barrier, inc=1, device_id=(p ^ m, b), device_id_type=MESH)
    load(2, "points", points, pts_v)
    load(2, "compress", compress, com_v)
    load(2, "top", top, top_v)
    late = (4, 6, 2, 1)
    waits = [((p >> bit) & 1 == 1) != (p < 8) for bit in (2, 2, 1, 0)]
    for m, waiter in zip(late, waits):
        @pl.when(jnp.logical_not(waiter))
        def _():
            pl.semaphore_signal(barrier, inc=1, device_id=(p ^ m, b), device_id_type=MESH)

    @pl.when(has_right)
    def _():
        pl.semaphore_signal(barrier, inc=1, device_id=(p, b + 1), device_id_type=MESH)


    def send(k, src, dst, to):
        c = pltpu.make_async_remote_copy(
            src_ref=src, dst_ref=dst, send_sem=ssem.at[0], recv_sem=rsem.at[k], device_id=to, device_id_type=MESH
        )
        c.start()
        return c

    loads["map"].wait()
    chosen, places = {}, {}

    def tables(j):
        chosen[j], places[j] = level_tables([map_s[j, i] for i in range(LEAVES)])
        for i in range(LEAVES):
            tab_s[j, i] = places[j][i]

    tables(0)

    loads["order"].wait()
    arrived(mix_v.at[pl.ds(0, 3), pl.ds(0, 3)], load_sem.at[2])
    load(3, "mixers", mixers, mix_v)
    load(4, "expand", expand, exp_v)
    load(4, "near", near, near_v)
    load(5, "neighbours", neighbours, near_s)
    chunks = [pts_v[:, pl.ds(k * LEAF, LEAF)].astype(F32) for k in range(LEAVES)]
    for s in range(SENT):
        c = chosen[0][s]
        row = ord_v[pl.ds(c, 1), :]
        rows = lane_gather(chunks, (row >> 7) & 7, row & 127).astype(BF)
        snd1[s] = stacked(dot(rows, com_v[c]))
    pl.semaphore_wait(barrier, 3 + sum(w.astype(jnp.int32) for w in (has_left, *waits)))
    send(0, snd1, rec1.at[1], (p ^ 24, b))
    send(0, snd1, rec1.at[0], (p ^ 16, b))
    tables(1)
    for s in range(SENT):
        top8_s[s] = top_v[chosen[1][s]]
    top_copy = send(1, top8_s, top8_r, (p ^ 8, b))
    for k, (m, waiter) in enumerate(zip(late, waits)):
        @pl.when(waiter)
        def _():
            pl.semaphore_signal(entered.at[k], inc=1, device_id=(p ^ m, b), device_id_type=MESH)

    def meet(k):
        @pl.when(jnp.logical_not(waits[k]))
        def _():
            pl.semaphore_wait(entered.at[k], 1)

    for j in range(2, 5):
        tables(j)
    for l in range(LEAVES):
        row = ord_v[pl.ds(l, 1), :]
        win[l + 2] = lane_gather(chunks, (row >> 7) & 7, row & 127).astype(BF)
    to_left = pltpu.make_async_remote_copy(
        src_ref=win.at[pl.ds(2, 2)], dst_ref=win.at[pl.ds(LEAVES + 2, 2)], send_sem=halo_ssem.at[0],
        recv_sem=halo_rsem.at[0], device_id=(p, b - 1), device_id_type=MESH,
    )
    to_right = pltpu.make_async_remote_copy(
        src_ref=win.at[pl.ds(LEAVES, 2)], dst_ref=win.at[pl.ds(0, 2)], send_sem=halo_ssem.at[1],
        recv_sem=halo_rsem.at[1], device_id=(p, b + 1), device_id_type=MESH,
    )

    @pl.when(has_left)
    def _():
        pl.semaphore_signal(entered.at[4], inc=1, device_id=(p, b - 1), device_id_type=MESH)
        to_left.start()

    @pl.when(jnp.logical_not(has_left))
    def _():
        win[0] = jnp.zeros((NV, LEAF), BF)
        win[1] = jnp.zeros((NV, LEAF), BF)

    @pl.when(jnp.logical_not(has_right))
    def _():
        win[LEAVES + 2] = jnp.zeros((NV, LEAF), BF)
        win[LEAVES + 3] = jnp.zeros((NV, LEAF), BF)
    loads["mixers"].wait()
    for s in range(SENT):
        mix2_s[s] = mix_v[1, chosen[3][s], 1]

    for i in range(LEAVES):
        w1[i] = paired(dot(top_v[i], mix_v[0, i, 0]))
    for i in range(LEAVES):
        w2[i, pl.ds(0, 2 * LEAF)] = paired(dot(mix_v[1, i].reshape(2 * LEAF, LEAF), mix_v[2, i, 0]))
    arrived(mix_v.at[pl.ds(0, 2)], load_sem.at[4])
    for i in range(LEAVES):
        w3[i] = paired(dot(mix_v[3, i].reshape(2 * LEAF, LEAF), exp_v[i]))
    sub = lax.broadcasted_iota(jnp.int32, (LEAVES, LEAF), 0)
    lane = lax.broadcasted_iota(jnp.int32, (LEAVES, LEAF), 1)
    tall = lax.broadcasted_iota(jnp.int32, (LEAF, LEAF), 0)
    table = jnp.zeros((2 * LEAVES, LEAF), F32)
    for l in range(LEAVES):
        row = ord_v[pl.ds(l, 1), :]
        here = jnp.broadcast_to((row >> 7) & 7, (LEAVES, LEAF)) == sub
        digits = jnp.concatenate(
            [jnp.where(here, float(l), 0.0), jnp.where(here, lane.astype(F32), 0.0)], axis=0
        ).astype(BF)
        spots = jnp.where(jnp.broadcast_to(row & 127, (LEAF, LEAF)) == tall, 1.0, 0.0).astype(BF)
        table += lax.dot_general(digits, spots, (((1,), (1,)), ((), ())), preferred_element_type=F32)
    inv_w[...] = table[:LEAVES].astype(jnp.int32)
    inv_l[...] = table[LEAVES:].astype(jnp.int32)

    meet(2)
    mix_copy = send(2, mix2_s, mix2_r, (p ^ 2, b))
    arrived(rec1, rsem.at[0])
    for i in range(LEAVES):
        own1[i] = apply_factor(rec1[0, places[0][i]], w1[i])
    top_copy.wait_recv()
    for s in range(SENT):
        part[s] = stacked(apply_exact(rec1[1, tab_s[0, chosen[1][s]]], top8_r[s]))

    def skeleton_2(c):
        return own1[c] + apply_exact(part[tab_s[1, c]], mix_v[0, c, 1])

    for s in range(SENT):
        snd2a[s] = stacked(skeleton_2(chosen[2][s]))
    meet(0)
    meet(1)
    send(3, snd2a, rec2.at[1], (p ^ 6, b))
    send(3, snd2a, rec2.at[0], (p ^ 4, b))
    for s in range(SENT):
        c = chosen[3][s]
        snd2b[s] = stacked(apply_exact(stacked(skeleton_2(c)), mix_v[1, c, 0]))
    send(3, snd2b, rec2.at[2], (p ^ 2, b))
    @pl.when(has_right)
    def _():
        pl.semaphore_wait(entered.at[4], 1)
        to_right.start()

    for i in range(LEAVES):
        st2[i] = stacked(skeleton_2(i))

    for i in range(LEAVES):
        acc[i] = apply_factor(st2[i], w2[i, pl.ds(0, LEAF)])
    mix_copy.wait_recv()
    for i in range(LEAVES):
        w2[i, pl.ds(2 * LEAF, LEAF)] = paired(dot(mix2_r[places[3][i]], mix_v[2, i, 1]))
    loads["neighbours"].wait()
    @pl.when(has_left)
    def _():
        to_right.wait_recv()

    @pl.when(has_right)
    def _():
        to_left.wait_recv()

    for i in range(LEAVES):
        rows = jnp.concatenate([win[jnp.clip(near_s[n, i] - me * LEAVES + 2, 0, LEAVES + 3)] for n in range(3)], axis=1)
        field[i] = dot(rows, near_v[i].reshape(3 * LEAF, LEAF))
    arrived(rec2, rsem.at[3])

    def skeleton_4(c):
        x = jnp.concatenate([rec2[0, tab_s[2, c]], rec2[1, tab_s[2, map_s[3, c]]]], axis=1)
        y = acc[c] + apply_exact(rec2[2, tab_s[3, c]], mix_v[2, c, 1])
        return y + apply_factor(x, w2[c, pl.ds(LEAF, 2 * LEAF)])

    for s in range(SENT):
        snd3[s] = stacked(skeleton_4(chosen[4][s]))
    meet(3)
    third = send(4, snd3, r1, (p ^ 1, b))
    for i in range(LEAVES):
        st4[i] = stacked(skeleton_4(i))
    for i in range(LEAVES):
        field[i] = field[i] + apply_factor(st4[i], w3[i, pl.ds(0, LEAF)])
    third.wait_recv()
    tree = []
    for i in range(LEAVES):
        tree.append(field[i] + apply_factor(r1[places[4][i]], w3[i, pl.ds(LEAF, LEAF)]))
    for l in range(LEAVES):
        out_ref[:, pl.ds(l * LEAF, LEAF)] = lane_gather(tree, inv_w[pl.ds(l, 1), :], inv_l[pl.ds(l, 1), :]).astype(BF)
    arrived(mix_v.at[pl.ds(0, 2), pl.ds(0, 5)], ssem.at[0])
    @pl.when(has_left)
    def _():
        to_left.wait_send()

    @pl.when(has_right)
    def _():
        to_right.wait_send()


def on_device(points, tree_order, near, neighbours, compress, expand, top, mixers, block_map):
    skeleton = pltpu.VMEM((SENT, 2 * NV, LEAF), BF)

    def received(count):
        return pltpu.VMEM((count, SENT, 2 * NV, LEAF), BF)

    return pl.pallas_call(
        kernel,
        out_shape=pltpu.VMEM(points.shape, points.dtype),
        in_specs=[pl.BlockSpec(memory_space=pltpu.HBM)] * 9,
        out_specs=pl.BlockSpec(memory_space=pltpu.VMEM),
        scratch_shapes=[
            pltpu.VMEM(points.shape, BF), pltpu.VMEM((LEAVES, LEAF), jnp.int32), pltpu.VMEM(near.shape, BF),
            pltpu.VMEM(compress.shape, BF), pltpu.VMEM(expand.shape, BF), pltpu.VMEM(top.shape, BF),
            pltpu.VMEM(mixers.shape, BF), pltpu.SMEM(neighbours.shape[::-1], jnp.int32), pltpu.SMEM(block_map.shape, jnp.int32),
            pltpu.SMEM(block_map.shape, jnp.int32),
            pltpu.VMEM((LEAVES + 4, NV, LEAF), BF), pltpu.VMEM((LEAVES, NV, LEAF), F32),
            pltpu.VMEM((LEAVES, LEAF), jnp.int32), pltpu.VMEM((LEAVES, LEAF), jnp.int32),
            pltpu.VMEM((LEAVES, NV, LEAF), F32),
            skeleton, received(2),
            pltpu.VMEM((SENT, LEAF, LEAF), BF), pltpu.VMEM((SENT, LEAF, LEAF), BF),
            pltpu.VMEM((SENT, LEAF, LEAF), BF), pltpu.VMEM((SENT, LEAF, LEAF), BF),
            skeleton, skeleton, received(3), skeleton, skeleton,
            pltpu.VMEM((LEAVES, LEAF, 2 * LEAF), BF), pltpu.VMEM((LEAVES, 3 * LEAF, 2 * LEAF), BF),
            pltpu.VMEM((LEAVES, 2 * LEAF, 2 * LEAF), BF),
            pltpu.VMEM((LEAVES, 2 * NV, LEAF), BF), pltpu.VMEM((LEAVES, 2 * NV, LEAF), BF),
            pltpu.VMEM((LEAVES, NV, LEAF), F32), skeleton,
            pltpu.SemaphoreType.DMA((6,)), pltpu.SemaphoreType.DMA((1,)), pltpu.SemaphoreType.DMA((5,)),
            pltpu.SemaphoreType.DMA((2,)), pltpu.SemaphoreType.DMA((2,)), pltpu.SemaphoreType.REGULAR((5,)),
        ],
        compiler_params=pltpu.CompilerParams(collective_id=0, has_side_effects=True, vmem_limit_bytes=58 * 2**20),
        cost_estimate=pl.CostEstimate(flops=200_000_000, bytes_accessed=4_000_000, transcendentals=0),
        name="butterfly",
    )(points, tree_order.reshape(LEAVES, LEAF), near, neighbours.T, compress, expand, top, mixers, block_map)


def solution(mesh):
    both = ("partner", "block")
    return jax.shard_map(
        on_device,
        mesh=mesh,
        in_specs=(
            P(None, both),
            P(both),
            P(both, None, None, None),
            P(both, None),
            P(both, None, None),
            P(both, None, None),
            P(both, None, None),
            P(None, both, None, None, None),
            P(),
        ),
        out_specs=P(None, both),
        check_vma=False,
    )
```
